32 devices in a mesh: section: 2 (over core), expert: 8 (over z, x), shard: 2 (over y).
Axes of the slice: x: 2, y: 2, z: 4, core: 2. Of those that a mesh axis runs over, the one named last changes fastest.
Arguments:
- stream: bfloat16 [2, 2048, 768], P(None, ('expert', 'shard')), may hold values from -6 to 6
- segments: int32 [2, 16, 128], P(None, ('expert', 'shard')), may hold values from 0 to 3, never falling along the last dimension, each value on 1 to 64 neighbouring positions
- routes: int32 [2, 2, 16, 128], P('section', None, ('expert', 'shard')), may hold values from 0 to 7, as said below
- room: int32 [2, 8], P('section'), may hold values from 12 to 24
- project_in: bfloat16 [2, 768, 2304], P('section', 'shard'), may hold values from -0.21875 to 0.21875
- project_out: bfloat16 [2, 768, 768], P('section', 'shard'), may hold values from -0.875 to 0.875
- bias_table: float32 [2, 32, 12], P('section'), may hold values from -6 to 6
- gain_mixer: float32 [2, 768], P('section'), may hold values from 0.5 to 1.5
- gain_expert: float32 [2, 768], P('section'), may hold values from 0.5 to 1.5
- router: bfloat16 [2, 768, 8], P('section', 'shard'), may hold values from -0.15625 to 0.15625
- expert_in: bfloat16 [2, 8, 3072, 768], P('section', 'expert'), may hold values from -0.21875 to 0.21875
- expert_out: bfloat16 [2, 8, 3072, 768], P('section', 'expert'), may hold values from -3 to 3
- cotangent: bfloat16 [2, 2048, 768], P(None, ('expert', 'shard')), may hold values from -6 to 6
Outputs:
- ends: float32 [2, 2, 2048, 768], P('section', None, ('expert', 'shard'))
- project_in_gradient: float32 [2, 768, 2304], P('section', ('expert', 'shard'))
- project_out_gradient: float32 [2, 768, 768], P('section', ('expert', 'shard'))
- table_gradient: float32 [2, 384], P('section', ('expert', 'shard'))
- gain_mixer_gradient: float32 [2, 768], P('section', ('expert', 'shard'))
- gain_expert_gradient: float32 [2, 768], P('section', ('expert', 'shard'))
- router_gradient: float32 [2, 768, 8], P('section', ('expert', 'shard'))
- expert_in_gradient: float32 [2, 8, 3072, 768], P('section', 'expert', 'shard')
- expert_out_gradient: float32 [2, 8, 3072, 768], P('section', 'expert', 'shard')
The draws below stay inside these ranges and needn't reach their ends.
Inputs may be any that keep to these rules, and one draw needn't show every extreme that they name: `routes`: in each layer one expert is named by 24 or more of the tokens of every sequence in every micro-batch.
All inputs are finite; a program needn't handle non-finite values.
Results may differ from the reference program's by a relative error of at most 0.025.
Values may be sent and summed in bfloat16 or wider, within the bound.
A program may use at most 192 MiB of HBM per device.

```python
import math
import jax
import jax.numpy as jnp
import numpy as np
from jax import lax

D = 768
H = 12
DH = 64
F = 3072
NB = 32
SEQ = 128
MB = 2
LAYERS = 2
E = 8
SEQS = 16
TOKENS = 2048
CAP = 24


def busy_experts(key):
    return jax.random.randint(key, (LAYERS,), 0, E)


def draw_routes(key, part):
    busy = busy_experts(key)
    key = jax.random.fold_in(key, 11)
    first, second = jax.random.split(key)
    count = LAYERS * MB * SEQS
    spare = jax.random.randint(first, (LAYERS, MB, SEQS, SEQ), 0, E)
    places = jnp.arange(SEQ, dtype=jnp.int32)
    layered = jnp.broadcast_to(busy[:, None, None, None], (LAYERS, MB, SEQS, SEQ))
    planned = jnp.where(places[None, None, None, :] < CAP, layered, spare).reshape(count, SEQ)
    orders = jax.vmap(lambda piece: jax.random.permutation(piece, SEQ))(jax.random.split(second, count))
    return jnp.take_along_axis(planned, orders, axis=1).reshape(LAYERS, MB, SEQS, SEQ).astype(jnp.int32)


def draw_room(key, part):
    busy = busy_experts(key)
    key = jax.random.fold_in(key, 12)
    spread = jax.random.randint(key, (LAYERS, E), CAP // 2, CAP + 1)
    labels = jnp.arange(E, dtype=jnp.int32)
    return jnp.where(labels[None, :] == busy[:, None], CAP, spread).astype(jnp.int32)


def levels(stream_key, shape, cuts, smallest, high):
    factor_of = 1.0
    for dim, parts in cuts:
        heights = jax.random.uniform(jax.random.fold_in(jax.random.fold_in(stream_key, 6), dim), (parts,), jnp.float32, smallest / len(cuts), high / len(cuts))
        factor_of = factor_of * jnp.repeat(jnp.exp(heights), shape[dim] // parts).reshape((-1,) + (1,) * (len(shape) - 1 - dim))
    return factor_of


def length_profile(amount, total, bound, slope):
    weights = [(1 << 20) // math.isqrt(grade ** slope) + 1 for grade in range(2, amount + 1)]
    rest, holding = total - bound - (amount - 1), [1] * (amount - 1)
    while rest > 0:
        movable = [i for i in range(amount - 1) if holding[i] < bound]
        mass, budget = sum([weights[i] for i in movable]), rest
        for i in movable:
            more = min(bound - holding[i], max(1, budget * weights[i] // mass), rest)
            holding[i] = holding[i] + more
            rest = rest - more
    return np.array([bound] + holding)


def uneven_parts(own_key, amount, total, most, skew):
    if amount == 2:
        one = jax.random.randint(own_key, (), max(1, total - most), min(most, total - 1) + 1)
        return jnp.stack([one, total - one])
    lengths = jnp.asarray(length_profile(amount, total, most, skew), jnp.int32)
    pairs = (amount - 1) // 2
    donor, receiver = lengths[1:1 + 2 * pairs:2], lengths[2:2 + 2 * pairs:2]
    slack = jnp.minimum(donor - 1, most - receiver)
    shifted = jax.random.randint(jax.random.fold_in(own_key, 1), (pairs,), 0, 1 << 20) % (slack + 1)
    lengths = lengths.at[1:1 + 2 * pairs:2].set(donor - shifted).at[2:2 + 2 * pairs:2].set(receiver + shifted)
    return lengths[jax.random.permutation(jax.random.fold_in(own_key, 2), amount)]


def bell_draw(rng, extent, deviation, reach, pieces=(), kind=jnp.bfloat16):
    array = deviation * jax.random.normal(rng, extent, jnp.float32)
    if pieces:
        array = array * levels(rng, extent, pieces, -0.22, 0.18)
    return jnp.clip(array, -reach, reach).astype(kind)


def setup_inputs(seed: int = 0) -> dict:
    splits = jax.random.split(jax.random.key(seed), 14)
    return {
        "stream": bell_draw(splits[0], (MB, TOKENS, D), 1.0, 6.0, ((1, 16),)),
        "segments": jax.vmap(lambda own: jnp.searchsorted(jnp.cumsum(uneven_parts(own, 4, SEQ, SEQ // 2, 1)), jnp.arange(SEQ), side="right"))(jax.random.split(splits[1], MB * SEQS)).reshape((MB, SEQS, SEQ)).astype(jnp.int32),
        "routes": draw_routes(jax.random.fold_in(splits[13], 71), 0),
        "room": draw_room(jax.random.fold_in(splits[13], 71), 0),
        "project_in": bell_draw(splits[4], (LAYERS, D, 3 * H * DH), D ** -0.5, 0.21875, ((0, 2), (1, 2))),
        "project_out": bell_draw(splits[5], (LAYERS, H * DH, D), (H * DH // 16) ** -0.5, 0.875, ((0, 2), (1, 2))),
        "bias_table": bell_draw(splits[6], (LAYERS, NB, H), 1.0, 6.0, ((0, 2),), jnp.float32),
        "gain_mixer": jnp.clip(1.0 + 0.1 * jax.random.normal(splits[7], (LAYERS, D), jnp.float32), 0.5, 1.5),
        "gain_expert": jnp.clip(1.0 + 0.1 * jax.random.normal(splits[8], (LAYERS, D), jnp.float32), 0.5, 1.5),
        "router": bell_draw(splits[9], (LAYERS, D, E), (2 * D) ** -0.5, 0.15625, ((0, 2), (1, 2))),
        "expert_in": bell_draw(splits[10], (LAYERS, E, F, D), D ** -0.5, 0.21875, ((0, 2), (1, 8))),
        "expert_out": bell_draw(splits[11], (LAYERS, E, F, D), (1.4 * E / F ** 0.5), 3.0, ((0, 2), (1, 8))),
        "cotangent": bell_draw(splits[12], (MB, TOKENS, D), 1.0, 6.0, ((1, 16),)),
    }


EPS = 1e-06
NEG = -1e+30
SPLITS = (12, 16, 23, 32, 46, 64, 91)
HIGHEST = lax.Precision.HIGHEST

@jax.custom_vjp
def low(v):
    return lax.optimization_barrier(v.astype(jnp.bfloat16)).astype(jnp.float32)

@jax.custom_vjp
def low_back(v):
    return v

def low_keep(v):
    return (low(v), None)

def low_pass(kept, grad):
    return (grad,)

def back_keep(v):
    return (v, None)

def back_low(kept, grad):
    return (low(grad),)
low.defvjp(low_keep, low_pass)
low_back.defvjp(back_keep, back_low)

def buckets(offset):
    span = jnp.abs(offset)
    far = 8 + sum(((span >= limit).astype(jnp.int32) for limit in SPLITS))
    return jnp.where(span < 8, span, far) + 16 * (offset > 0).astype(jnp.int32)

def normalize(values, gain):
    return values * lax.rsqrt(lax.optimization_barrier(jnp.mean(values * values, axis=-1, keepdims=True)) + EPS) * gain

def attention(normed, marks, bias, mix_in, mix_out):
    group = math.gcd(SEQS, max(1, 4096 // SEQ))
    blocks = SEQS // group
    rows = normed.reshape(blocks, group, SEQ, D)
    labels = marks.reshape(blocks, group, SEQ)

    def block(pair):
        rows_here, marks_here = pair
        packed = jnp.einsum('gsd,de->gse', rows_here, mix_in, precision=HIGHEST)
        packed = low_back(low(packed)).reshape(group, SEQ, 3, H, DH)
        queries, keys, values = (packed[:, :, 0], packed[:, :, 1], packed[:, :, 2])
        scores = jnp.einsum('gqhc,gkhc->ghqk', queries, keys, precision=HIGHEST) * DH ** (-0.5) + bias[None]
        scores = low_back(scores)
        same = marks_here[:, None, :, None] == marks_here[:, None, None, :]
        scores = jnp.where(same, scores, NEG)
        probs = low(jax.nn.softmax(scores, axis=-1))
        mixed = jnp.einsum('ghqk,gkhc->gqhc', probs, values, precision=HIGHEST).reshape(group, SEQ, H * DH)
        mixed = low_back(low(mixed))
        return low_back(jnp.einsum('gsi,id->gsd', mixed, mix_out, precision=HIGHEST))
    return lax.map(jax.checkpoint(block), (rows, labels)).reshape(SEQS, SEQ, D)

def experts(second, chosen, room, expert_in, expert_out):
    picks = chosen[..., None] == jnp.arange(E, dtype=jnp.int32)
    counts = jnp.cumsum(picks.astype(jnp.int32), axis=1) - 1
    order = lax.optimization_barrier(jnp.sum(jnp.where(picks, counts, 0), axis=-1))
    limit = room[chosen]
    slots = jnp.where(order < limit, chosen * CAP + order, E * CAP).astype(jnp.int32)
    lines = jnp.broadcast_to(jnp.arange(SEQS, dtype=jnp.int32)[:, None], (SEQS, SEQ))
    buffer = jnp.zeros((SEQS, E * CAP + 1, D), jnp.float32).at[lines, slots].set(second)
    sending = buffer[:, :E * CAP].reshape(SEQS, E, CAP, D).transpose(1, 0, 2, 3).reshape(E, SEQS * CAP, D)
    sending = low_back(sending)

    def apply(trio):
        rows, weight_in, weight_out = trio
        before = low_back(jnp.dot(rows, weight_in.T, precision=HIGHEST))
        hidden = low(jax.nn.gelu(before))
        return low_back(low(jnp.dot(hidden, weight_out, precision=HIGHEST)))
    output = lax.map(jax.checkpoint(apply), (sending, expert_in, expert_out))
    output = output.reshape(E, SEQS, CAP, D).transpose(1, 0, 2, 3).reshape(SEQS, E * CAP, D)
    output = jnp.concatenate([output, jnp.zeros((SEQS, 1, D), jnp.float32)], axis=1)
    return (jnp.take_along_axis(output, slots[..., None], axis=1), picks)

def section_layer(stream, marks, chosen, room, mix_in, mix_out, table, gain_mixer, gain_expert, router, expert_in, expert_out):
    places = jnp.arange(SEQ, dtype=jnp.int32)
    bias = jnp.transpose(table[buckets(places[None, :] - places[:, None])], (2, 0, 1))
    normed = low(normalize(stream, gain_mixer))
    middle = stream + attention(normed, marks, bias, mix_in, mix_out)
    second = low(normalize(middle, gain_expert))
    logits = low_back(jnp.einsum('sqd,de->sqe', second, router, precision=HIGHEST))
    chances = jax.nn.softmax(logits, axis=-1)
    picked, picks = experts(second, chosen, room, expert_in, expert_out)
    gate = lax.optimization_barrier(jnp.sum(jnp.where(picks, chances, 0.0), axis=-1))
    return middle + gate[..., None] * picked

def reference(stream, segments, routes, room, project_in, project_out, bias_table, gain_mixer, gain_expert, router, expert_in, expert_out, cotangent):

    def model(inputs, mix_in, mix_out, table, gains_first, gains_second, routing, weights_in, weights_out):
        finals = []
        for index in range(MB):
            current = inputs[index].reshape(SEQS, SEQ, D)
            for layer in range(LAYERS):
                if layer > 0:
                    current = low_back(low(current))
                current = section_layer(current, segments[index], routes[layer, index], room[layer], mix_in[layer], mix_out[layer], table[layer], gains_first[layer], gains_second[layer], routing[layer], weights_in[layer], weights_out[layer])
            finals.append(current.reshape(TOKENS, D))
        return jnp.stack(finals)
    floats = (stream, project_in, project_out, bias_table, gain_mixer, gain_expert, router, expert_in, expert_out)
    floats = tuple((value.astype(jnp.float32) for value in floats))
    final, pull = jax.vjp(model, *floats)
    grads = pull(cotangent.astype(jnp.float32))
    ends = jnp.stack([grads[0], final])
    return (ends, grads[1], grads[2], grads[3].reshape(LAYERS, NB * H), grads[4], grads[5], grads[6], grads[7], grads[8])
```

```python
import functools

import jax
import jax.numpy as jnp
from jax import lax
from jax.experimental import pallas as pl
from jax.experimental.pallas import tpu as pltpu
from jax.sharding import PartitionSpec as P

EPS = 1e-06
NEG = -1e30
SPLITS = (12, 16, 23, 32, 46, 64, 91)
HIGHEST = lax.Precision.HIGHEST
F32 = jnp.float32
BF16 = jnp.bfloat16
GELU_A = 0.7978845608028654
GELU_B = 0.044715
VMEM = 48 * 1024 * 1024


def dot(a, b):
    return lax.dot_general(a, b, (((1,), (0,)), ((), ())), preferred_element_type=F32)


def dot_nt(a, b):
    return lax.dot_general(a, b, (((1,), (1,)), ((), ())), preferred_element_type=F32)


def dot_tn(a, b):
    return lax.dot_general(a, b, (((0,), (0,)), ((), ())), preferred_element_type=F32)


def gelu_parts(v):
    th = jnp.tanh(GELU_A * (v + GELU_B * v * v * v))
    return 0.5 * v * (1.0 + th), th


def gelu_slope(v, th):
    return 0.5 * (1.0 + th) + 0.5 * v * (1.0 - th * th) * (GELU_A * (1.0 + 3.0 * GELU_B * v * v))


def buckets(offset):
    span = jnp.abs(offset)
    far = 8 + sum(((span >= limit).astype(jnp.int32) for limit in SPLITS))
    return jnp.where(span < 8, span, far) + 16 * (offset > 0).astype(jnp.int32)


def load_weights(flags, own_m, own_p, oth_m, oth_p, held, sems):
    half = own_m.shape[0]
    y = flags[1]
    low = pl.ds(pl.multiple_of(y * half, half), half)
    high = pl.ds(pl.multiple_of((1 - y) * half, half), half)

    def both(first, second):
        a = pltpu.make_async_copy(first, held.at[low], sems.at[0])
        b = pltpu.make_async_copy(second, held.at[high], sems.at[1])
        a.start()
        b.start()
        a.wait()
        b.wait()

    @pl.when(flags[0] == 1)
    def _():
        both(own_m, own_p)

    @pl.when(flags[0] == 0)
    def _():
        both(oth_m, oth_p)


def bias_of(along, head, length):
    wide = jnp.broadcast_to(along[head : head + 1, :], (length, 2 * length))
    return pltpu.roll(wide, length + 1, 1, stride=1, stride_axis=0)[:, :length]


def probs_of(q, k2, scale, bias, same):
    scores = dot_nt(q, k2) * scale + bias
    scores = jnp.where(same, scores, NEG)
    peak = jnp.max(scores, axis=-1, keepdims=True)
    raised = jnp.exp(scores - peak)
    return raised / jnp.sum(raised, axis=-1, keepdims=True)


def mixer_fwd(heads, experts, flags, h_ref, gm_ref, ge_ref, along_ref, mcol, mrow, srow, own_m, own_p,
              oth_m, oth_p, packed_ref, mixed_ref, middle_ref, second_ref, chances_ref, send_ref, held, sems):
    load_weights(flags, own_m, own_p, oth_m, oth_p, held, sems)
    length, d = h_ref.shape
    h = h_ref[...]
    s = lax.rsqrt(jnp.mean(h * h, axis=-1, keepdims=True) + EPS)
    normed = (h * s * gm_ref[...]).astype(BF16)
    packed_ref[...] = dot(normed, held[:, : 3 * d]).astype(BF16)
    size = d // heads
    scale = size ** (-0.5)
    same = mcol[...] == mrow[...]
    low = lax.broadcasted_iota(jnp.int32, (length, 2 * size), 1) < size
    for pair in range(heads // 2):
        at = slice(2 * size * pair, 2 * size * (pair + 1))
        q2 = packed_ref[:, at]
        k2 = packed_ref[:, d + at.start : d + at.stop]
        v2 = packed_ref[:, 2 * d + at.start : 2 * d + at.stop]
        zero = jnp.zeros_like(q2)
        pa = probs_of(jnp.where(low, q2, zero), k2, scale, bias_of(along_ref, 2 * pair, length), same)
        pb = probs_of(jnp.where(low, zero, q2), k2, scale, bias_of(along_ref, 2 * pair + 1, length), same)
        mixed_ref[:, at] = jnp.where(low, dot(pa.astype(BF16), v2), dot(pb.astype(BF16), v2)).astype(BF16)
    middle = h + dot(mixed_ref[...], held[:, 3 * d : 4 * d])
    middle_ref[...] = middle
    r = lax.rsqrt(jnp.mean(middle * middle, axis=-1, keepdims=True) + EPS)
    second = (middle * r * ge_ref[...]).astype(BF16)
    second_ref[...] = second
    logits = dot(second, held[:, 4 * d :])
    lanes = lax.broadcasted_iota(jnp.int32, logits.shape, 1)
    logits = jnp.where(lanes < experts, logits, NEG)
    raised = jnp.exp(logits - jnp.max(logits, axis=-1, keepdims=True))
    chances_ref[...] = raised / jnp.sum(raised, axis=-1, keepdims=True)
    slots = send_ref.shape[0]
    hot = (lax.broadcasted_iota(jnp.int32, (slots, length), 0) == srow[...]).astype(F32).astype(BF16)
    send_ref[...] = dot(hot, second).astype(BF16)


def mixer_bwd(heads, flags, g_ref, h_ref, middle_ref, second_ref, packed_ref, mixed_ref, gm_ref, ge_ref,
              along_ref, mcol, mrow, scol, dlog_ref, ret_ref, own_m, own_p, oth_m, oth_p,
              dh_ref, grad_ref, tail_ref, gains_ref, diag_ref, held, dpacked, sems):
    load_weights(flags, own_m, own_p, oth_m, oth_p, held, sems)
    length, d = h_ref.shape
    slots = ret_ref.shape[0]
    g = g_ref[...]
    dlog = dlog_ref[...]
    second = second_ref[...]
    hot = (lax.broadcasted_iota(jnp.int32, (length, slots), 1) == scol[...]).astype(F32).astype(BF16)
    dsecond = dot_nt(dlog, held[:, 4 * d :]) + dot(hot, ret_ref[...])
    tail_ref[...] = dot_tn(second, dlog)
    middle = middle_ref[...]
    r = lax.rsqrt(jnp.mean(middle * middle, axis=-1, keepdims=True) + EPS)
    t = dsecond * ge_ref[...]
    dge = jnp.sum(dsecond * middle * r, axis=0, keepdims=True)
    dmiddle = g + r * t - middle * (r * r * r) * jnp.mean(middle * t, axis=-1, keepdims=True)
    dbranch = dmiddle.astype(BF16)
    grad_ref[:, 3 * d :] = dot_tn(mixed_ref[...], dbranch).astype(BF16)
    dmixed = dot_nt(dbranch, held[:, 3 * d : 4 * d]).astype(BF16)
    size = d // heads
    scale = size ** (-0.5)
    same = mcol[...] == mrow[...]
    low = lax.broadcasted_iota(jnp.int32, (length, 2 * size), 1) < size
    for pair in range(heads // 2):
        at = slice(2 * size * pair, 2 * size * (pair + 1))
        q2 = packed_ref[:, at]
        k2 = packed_ref[:, d + at.start : d + at.stop]
        v2 = packed_ref[:, 2 * d + at.start : 2 * d + at.stop]
        dm2 = dmixed[:, at]
        zero = jnp.zeros_like(q2)
        parts = []
        for which in range(2):
            mine = low if which == 0 else jnp.logical_not(low)
            head = 2 * pair + which
            p = probs_of(jnp.where(mine, q2, zero), k2, scale, bias_of(along_ref, head, length), same)
            dp = dot_nt(jnp.where(mine, dm2, zero), v2)
            ds = (p * (dp - jnp.sum(dp * p, axis=-1, keepdims=True))).astype(BF16)
            parts.append((dot(ds, k2), dot_tn(ds, q2), dot_tn(p.astype(BF16), dm2)))
            diag_ref[head] = ds
        dpacked[:, at] = (jnp.where(low, parts[0][0], parts[1][0]) * scale).astype(BF16)
        dpacked[:, d + at.start : d + at.stop] = (jnp.where(low, parts[0][1], parts[1][1]) * scale).astype(BF16)
        dpacked[:, 2 * d + at.start : 2 * d + at.stop] = jnp.where(low, parts[0][2], parts[1][2]).astype(BF16)
    h = h_ref[...]
    s = lax.rsqrt(jnp.mean(h * h, axis=-1, keepdims=True) + EPS)
    normed = (h * s * gm_ref[...]).astype(BF16)
    grad_ref[:, : 3 * d] = dot_tn(normed, dpacked[...]).astype(BF16)
    dnormed = dot_nt(dpacked[...], held[:, : 3 * d])
    u = dnormed * gm_ref[...]
    dgm = jnp.sum(dnormed * h * s, axis=0, keepdims=True)
    dh_ref[...] = dmiddle + s * u - h * (s * s * s) * jnp.mean(h * u, axis=-1, keepdims=True)
    gains_ref[0:1, :] = dgm
    gains_ref[1:2, :] = dge


def ffn_fwd(flags, rows_ref, wi_own, wo_own, wi_oth, wo_oth, out_ref, acc):
    step = pl.program_id(0)

    @pl.when(step == 0)
    def _():
        acc[...] = jnp.zeros_like(acc)

    def work(wi, wo):
        hidden = gelu_parts(dot_nt(rows_ref[...], wi[...]))[0].astype(BF16)
        acc[...] += dot(hidden, wo[...])

    @pl.when(flags[0] == 1)
    def _():
        work(wi_own, wo_own)

    @pl.when(flags[0] == 0)
    def _():
        work(wi_oth, wo_oth)

    @pl.when(step == pl.num_programs(0) - 1)
    def _():
        out_ref[...] = acc[...].astype(BF16)


def ffn_bwd(flags, rows_ref, pull_ref, wi_own, wo_own, wi_oth, wo_oth, out_ref, acc):
    step = pl.program_id(0)

    @pl.when(step == 0)
    def _():
        acc[...] = jnp.zeros_like(acc)

    def work(wi, wo):
        before = dot_nt(rows_ref[...], wi[...])
        th = gelu_parts(before)[1]
        slope = (gelu_slope(before, th) * dot_nt(pull_ref[...], wo[...])).astype(BF16)
        acc[...] += dot(slope, wi[...])

    @pl.when(flags[0] == 1)
    def _():
        work(wi_own, wo_own)

    @pl.when(flags[0] == 0)
    def _():
        work(wi_oth, wo_oth)

    @pl.when(step == pl.num_programs(0) - 1)
    def _():
        out_ref[...] = acc[...].astype(BF16)


def weight_grads(flags, rows_ref, pull_ref, wi, wo, gin_ref, gout_ref):
    rows = rows_ref[...]
    pulls = pull_ref[...]
    before = dot_nt(rows, wi[...])
    act, th = gelu_parts(before)
    slope = (gelu_slope(before, th) * dot_nt(pulls, wo[...])).astype(BF16)
    gout_ref[...] = dot_tn(act.astype(BF16), pulls)
    gin_ref[...] = dot_tn(slope, rows)


def call_ffn(kernel, flags, arrays, own, oth):
    rows, d = arrays[0].shape
    f = own[0].shape[0]
    block = 512 if f % 512 == 0 else f
    whole = pl.BlockSpec((rows, d), lambda i, s: (0, 0))
    mine = pl.BlockSpec((block, d), lambda i, s: (i * s[0], 0))
    theirs = pl.BlockSpec((block, d), lambda i, s: (i * (1 - s[0]), 0))
    n = len(arrays)
    return pl.pallas_call(
        kernel,
        out_shape=jax.ShapeDtypeStruct((rows, d), BF16),
        grid_spec=pltpu.PrefetchScalarGridSpec(
            num_scalar_prefetch=1,
            grid=(f // block,),
            in_specs=[whole] * n + [mine, mine, theirs, theirs],
            out_specs=whole,
            scratch_shapes=[pltpu.VMEM((rows, d), F32)],
        ),
        compiler_params=pltpu.CompilerParams(vmem_limit_bytes=VMEM),
        cost_estimate=pl.CostEstimate(
            flops=4 * n * rows * d * f, bytes_accessed=4 * f * d + 4 * rows * d, transcendentals=rows * f
        ),
    )(flags, *arrays, *own, *oth)


def call_grads(flags, rows, pulls, wi, wo):
    count, d = rows.shape
    f = wi.shape[0] // 2
    block = 256
    steps = f // block
    whole = pl.BlockSpec((count, d), lambda i, s: (0, 0))
    part = pl.BlockSpec((block, d), lambda i, s: (s[1] * steps + i, 0))
    out = pl.BlockSpec((block, d), lambda i, s: (i, 0))
    return pl.pallas_call(
        weight_grads,
        out_shape=[jax.ShapeDtypeStruct((f, d), F32)] * 2,
        grid_spec=pltpu.PrefetchScalarGridSpec(
            num_scalar_prefetch=1,
            grid=(steps,),
            in_specs=[whole, whole, part, part],
            out_specs=[out, out],
        ),
        compiler_params=pltpu.CompilerParams(vmem_limit_bytes=VMEM),
        cost_estimate=pl.CostEstimate(
            flops=8 * count * d * f, bytes_accessed=12 * f * d, transcendentals=count * f
        ),
    )(flags, rows, pulls, wi, wo)


def call_mixer(kernel, flags, arrays, weights, outs, extra):
    vm = pl.BlockSpec(memory_space=pltpu.VMEM)
    half, cols = weights[0].shape
    return pl.pallas_call(
        kernel,
        out_shape=[jax.ShapeDtypeStruct(shape, kind) for shape, kind in outs],
        in_specs=[pl.BlockSpec(memory_space=pltpu.SMEM)]
        + [vm] * len(arrays)
        + [pl.BlockSpec(memory_space=pl.ANY)] * 4,
        out_specs=[vm] * len(outs),
        scratch_shapes=[pltpu.VMEM((2 * half, cols), BF16)] + extra + [pltpu.SemaphoreType.DMA((2,))],
        compiler_params=pltpu.CompilerParams(vmem_limit_bytes=VMEM),
        cost_estimate=pl.CostEstimate(
            flops=3 * 10**9, bytes_accessed=10**7, transcendentals=10**5
        ),
    )(flags, *arrays, *weights)


def swap(x, axis):
    return lax.ppermute(x, axis, [(0, 1), (1, 0)])


def only(x, axis, layer, by):
    n = lax.axis_size(axis)
    return lax.ppermute(x, ("section", axis), [(layer * n + i, layer * n + (i ^ by)) for i in range(n)])


def across(x, layer):
    return lax.ppermute(x, "section", [(1 - layer, layer)])


def reduce_rows(grad, layer, order):
    n = lax.axis_size("expert")
    bits = n.bit_length() - 1
    e, y = lax.axis_index("expert"), lax.axis_index("shard")
    left = list(range(bits + 1))
    dims = [2] * (bits + 1)
    part = grad.reshape(*dims, grad.shape[0] // (2 * n), grad.shape[1])
    for dim in order(bits):
        at = left.index(dim)
        left.remove(dim)
        if dim == bits:
            bit, axis, by = y, "shard", 1
        else:
            by = 1 << (bits - 1 - dim)
            bit, axis = (e // by) % 2, "expert"
        keep = lax.dynamic_index_in_dim(part, bit, at, keepdims=False)
        send = lax.dynamic_index_in_dim(part, 1 - bit, at, keepdims=False)
        got = only(send, axis, layer, by)
        part = (keep.astype(F32) + got.astype(F32)).astype(part.dtype if left else F32)
    return part


def order_a(bits):
    return [bits, bits - 1] + list(range(bits - 1))


def order_b(bits):
    return [bits - 1] + list(range(bits - 1)) + [bits]


def order_c(bits):
    return list(range(bits - 1)) + [bits, bits - 1]


def exchange(x, n):
    slots, d = x.shape
    return lax.all_to_all(
        x.reshape(n, slots // n, d), "expert", split_axis=0, concat_axis=0, tiled=True
    ).reshape(slots, d)


def shards(
    stream, segments, routes, room, project_in, project_out, bias_table, gain_mixer, gain_expert,
    router, expert_in, expert_out, cotangent,
):
    c = lax.axis_index("section")
    y = lax.axis_index("shard")
    n = lax.axis_size("expert")
    length, d = stream.shape[1:]
    heads = bias_table.shape[2]
    labels_n = bias_table.shape[1]
    experts = router.shape[2]
    capacity = max(2, 3 * length // (2 * experts))
    slots_all = experts * capacity
    table_size = labels_n * heads

    joined = jnp.concatenate(
        [project_in[0], project_out[0], jnp.pad(router[0], ((0, 0), (0, 128 - experts)))], axis=1
    )
    peer0 = only(joined, "shard", 0, 1)
    over0 = (across(joined, 1), across(peer0, 1))
    wi, wo = expert_in[0, 0], expert_out[0, 0]
    small = jnp.concatenate(
        [bias_table[0].reshape(-1), gain_mixer[0], gain_expert[0], room[0].astype(F32)]
    )
    small_other = swap(small, "section")
    route_here = lax.dynamic_index_in_dim(routes[0], c, 0, keepdims=False)[0]
    route_other = swap(lax.dynamic_index_in_dim(routes[0], 1 - c, 0, keepdims=False)[0], "section")
    wi_other, wo_other = swap(wi, "section"), swap(wo, "section")
    peer1 = only(joined, "shard", 1, 1)
    over1 = (across(joined, 0), across(peer1, 0))
    weights = (
        (joined, peer0, over0[0], over0[1]),
        (joined, peer1, over1[0], over1[1]),
    )
    marks = lax.dynamic_index_in_dim(segments, c, 0, keepdims=False)
    mcol, mrow = marks.reshape(length, 1), marks.reshape(1, length)
    offsets = jnp.arange(2 * length, dtype=jnp.int32) - (length - 1)
    hits = (buckets(offsets)[:, None] == jnp.arange(labels_n, dtype=jnp.int32)[None, :]).astype(F32)

    given = []
    for layer in range(2):
        mine = c == layer
        flags = jnp.stack([mine.astype(jnp.int32), y.astype(jnp.int32)])
        values = jnp.where(mine, small, small_other)
        table = values[:table_size].reshape(labels_n, heads)
        gm = values[table_size : table_size + d].reshape(1, d)
        ge = values[table_size + d : table_size + 2 * d].reshape(1, d)
        limits = values[table_size + 2 * d :].astype(jnp.int32)
        chosen = jnp.where(mine, route_here, route_other)
        along = jnp.dot(table.T, hits.T, precision=HIGHEST)
        picks = chosen[:, None] == jnp.arange(experts, dtype=jnp.int32)[None, :]
        earlier = jnp.tril(jnp.ones((length, length), BF16), -1)
        counts = dot(earlier, picks.astype(BF16)).astype(jnp.int32)
        rank = jnp.sum(jnp.where(picks, counts, 0), axis=-1)
        limit = jnp.sum(jnp.where(picks, limits[None, :], 0), axis=-1)
        slots = jnp.where(rank < limit, chosen * capacity + rank, slots_all)
        given.append((flags, gm, ge, along, chosen, slots))

    current = lax.dynamic_index_in_dim(stream, c, 0, keepdims=False).astype(F32)
    saved = []
    for layer in range(2):
        flags, gm, ge, along, chosen, slots = given[layer]
        scol, srow = slots.reshape(length, 1), slots.reshape(1, length)
        packed, mixed, middle, second, chances, sending = call_mixer(
            functools.partial(mixer_fwd, heads, experts),
            flags,
            (current, gm, ge, along, mcol, mrow, srow),
            weights[layer],
            [
                ((length, 3 * d), BF16),
                ((length, d), BF16),
                ((length, d), F32),
                ((length, d), BF16),
                ((length, 128), F32),
                ((slots_all, d), BF16),
            ],
            [],
        )
        rows = exchange(sending, n)
        output = call_ffn(ffn_fwd, flags, (rows,), (wi, wo), (wi_other, wo_other))
        back = exchange(output, n)
        hot = (jnp.arange(slots_all, dtype=jnp.int32)[None, :] == scol).astype(BF16)
        picked = dot(hot, back)
        lane = jnp.arange(128, dtype=jnp.int32)[None, :] == chosen[:, None]
        gate = jnp.sum(jnp.where(lane, chances, 0.0), axis=-1, keepdims=True)
        result = middle + gate * picked
        saved.append((current, packed, mixed, middle, second, chances, rows, picked, gate, lane))
        current = result.astype(BF16).astype(F32)
    final = result

    rows_mine = jnp.where(c == 0, saved[0][6], saved[1][6])
    rows_sent = swap(jnp.where(c == 0, saved[1][6], saved[0][6]), "section")
    rows_pair = jnp.concatenate([rows_mine, rows_sent], axis=0)
    rows_all = jnp.concatenate([rows_pair, swap(rows_pair, "shard")], axis=0)

    pull = lax.dynamic_index_in_dim(cotangent, c, 0, keepdims=False).astype(F32)
    pulls = [None, None]
    reduced = [None, None]
    for layer in (1, 0):
        flags, gm, ge, along, chosen, slots = given[layer]
        inputs, packed, mixed, middle, second, chances, rows, picked, gate, lane = saved[layer]
        scol, srow = slots.reshape(length, 1), slots.reshape(1, length)
        pull_gate = jnp.sum(pull * picked, axis=-1, keepdims=True)
        pull_logits = (chances * (jnp.where(lane, pull_gate, 0.0) - pull_gate * gate)).astype(BF16)
        pull_picked = (gate * pull).astype(BF16)
        hot = (jnp.arange(slots_all, dtype=jnp.int32)[:, None] == srow).astype(BF16)
        pulls[layer] = exchange(dot(hot, pull_picked).astype(BF16), n)
        back_rows = call_ffn(ffn_bwd, flags, (rows, pulls[layer]), (wi, wo), (wi_other, wo_other))
        returned = exchange(back_rows, n)
        d_inputs, grad, tail, gains, grid = call_mixer(
            functools.partial(mixer_bwd, heads),
            flags,
            (pull, inputs, middle, second, packed, mixed, gm, ge, along, mcol, mrow, scol, pull_logits, returned),
            weights[layer],
            [
                ((length, d), F32),
                ((d, 4 * d), BF16),
                ((d, 128), F32),
                ((8, d), F32),
                ((heads, length, length), BF16),
            ],
            [pltpu.VMEM((length, 3 * d), BF16)],
        )
        places = jnp.arange(length, dtype=jnp.int32)
        which = buckets(places[None, :] - places[:, None])
        each = (which[None] == jnp.arange(labels_n, dtype=jnp.int32)[:, None, None]).astype(BF16)
        grad_table = jnp.einsum("bij,hij->bh", each, grid, preferred_element_type=F32)
        devices = 2 * n
        padded = jnp.pad(
            grad_table.reshape(devices, -1), ((0, 0), (0, d // devices - table_size // devices))
        ) if d // devices >= table_size // devices else None
        smalls = jnp.stack([gains[0], gains[1], padded.reshape(d)], axis=1)
        tail = jnp.concatenate([tail[:, :experts], smalls, jnp.zeros((d, 125 - experts), F32)], axis=1)
        third = 4 * d // 3
        pieces = []
        for index, order in enumerate((order_a, order_b, order_c)):
            piece = grad[:, index * third : (index + 1) * third]
            summed = (piece.astype(F32) + across(piece, layer).astype(F32)).astype(BF16)
            pieces.append(reduce_rows(summed, layer, order))
        tail = tail + across(tail, layer)
        pieces.append(reduce_rows(tail, layer, order_b))
        reduced[layer] = jnp.concatenate(pieces, axis=1)
        pull = d_inputs.astype(BF16).astype(F32)

    pull_mine = jnp.where(c == 0, pulls[0], pulls[1])
    pull_sent = swap(jnp.where(c == 0, pulls[1], pulls[0]), "section")
    pull_pair = jnp.concatenate([pull_mine, pull_sent], axis=0)
    pull_all = jnp.concatenate([pull_pair, swap(pull_pair, "shard")], axis=0)
    grad_in, grad_out = call_grads(given[0][0], rows_all, pull_all, wi, wo)

    got = swap(jnp.where(c == 0, final, d_inputs), "section")
    ends = jnp.stack([jnp.where(c == 0, d_inputs, got), jnp.where(c == 0, got, final)])
    total = jnp.where(c == 0, reduced[0], reduced[1])
    at = 4 * d + experts
    share = table_size // (2 * n)
    return (
        ends[None],
        total[None, :, : 3 * d],
        total[None, :, 3 * d : 4 * d],
        total[None, :share, at + 2],
        total[None, :, at],
        total[None, :, at + 1],
        total[None, :, 4 * d : at],
        grad_in[None, None],
        grad_out[None, None],
    )


def solution(mesh):
    placed = (
        P(None, ("expert", "shard"), None),
        P(None, ("expert", "shard"), None),
        P("section", None, ("expert", "shard"), None),
        P("section", None),
        P("section", "shard", None),
        P("section", "shard", None),
        P("section", None, None),
        P("section", None),
        P("section", None),
        P("section", "shard", None),
        P("section", "expert", None, None),
        P("section", "expert", None, None),
        P(None, ("expert", "shard"), None),
    )
    return jax.shard_map(
        shards,
        mesh=mesh,
        in_specs=placed,
        out_specs=(
            P("section", None, ("expert", "shard"), None),
            P("section", ("expert", "shard"), None),
            P("section", ("expert", "shard"), None),
            P("section", ("expert", "shard")),
            P("section", ("expert", "shard")),
            P("section", ("expert", "shard")),
            P("section", ("expert", "shard"), None),
            P("section", "expert", "shard", None),
            P("section", "expert", "shard", None),
        ),
        check_vma=False,
    )
```

```python
import functools

import jax
import jax.numpy as jnp
from jax import lax
from jax.experimental import pallas as pl
from jax.experimental.pallas import tpu as pltpu
from jax.sharding import PartitionSpec as P

EPS = 1e-06
NEG = -1e30
SPLITS = (12, 16, 23, 32, 46, 64, 91)
HIGHEST = lax.Precision.HIGHEST
F32 = jnp.float32
BF16 = jnp.bfloat16
GELU_A = 0.7978845608028654
GELU_B = 0.044715
VMEM = 48 * 1024 * 1024


def dot(a, b):
    return lax.dot_general(a, b, (((1,), (0,)), ((), ())), preferred_element_type=F32)


def dot_nt(a, b):
    return lax.dot_general(a, b, (((1,), (1,)), ((), ())), preferred_element_type=F32)


def dot_tn(a, b):
    return lax.dot_general(a, b, (((0,), (0,)), ((), ())), preferred_element_type=F32)


def gelu_parts(v):
    th = jnp.tanh(GELU_A * (v + GELU_B * v * v * v))
    return 0.5 * v * (1.0 + th), th


def gelu_slope(v, th):
    return 0.5 * (1.0 + th) + 0.5 * v * (1.0 - th * th) * (GELU_A * (1.0 + 3.0 * GELU_B * v * v))


def buckets(offset):
    span = jnp.abs(offset)
    far = 8 + sum(((span >= limit).astype(jnp.int32) for limit in SPLITS))
    return jnp.where(span < 8, span, far) + 16 * (offset > 0).astype(jnp.int32)


def load_weights(flags, refs, held, rest, sems):
    half = refs[0].shape[0]
    y = flags[1]
    low = pl.ds(pl.multiple_of(y * half, half), half)
    high = pl.ds(pl.multiple_of((1 - y) * half, half), half)

    def all_four(sources):
        places = (held.at[low], held.at[high], rest.at[low], rest.at[high])
        copies = [pltpu.make_async_copy(a, b, sems.at[i]) for i, (a, b) in enumerate(zip(sources, places))]
        for copy in copies:
            copy.start()
        for copy in copies:
            copy.wait()

    @pl.when(flags[0] == 1)
    def _():
        all_four((refs[0], refs[1], refs[4], refs[5]))

    @pl.when(flags[0] == 0)
    def _():
        all_four((refs[2], refs[3], refs[6], refs[7]))


def bias_of(along, head, length):
    wide = jnp.broadcast_to(along[head : head + 1, :], (length, 2 * length))
    return pltpu.roll(wide, length + 1, 1, stride=1, stride_axis=0)[:, :length]


def probs_of(q, k2, scale, bias, same):
    scores = dot_nt(q, k2) * scale + bias
    scores = jnp.where(same, scores, NEG)
    peak = jnp.max(scores, axis=-1, keepdims=True)
    raised = jnp.exp(scores - peak)
    return raised / jnp.sum(raised, axis=-1, keepdims=True)


def mixer_fwd(heads, experts, flags, h_ref, gm_ref, ge_ref, along_ref, mcol, mrow, srow, w0, w1, w2, w3,
              w4, w5, w6, w7, packed_ref, mixed_ref, middle_ref, second_ref, chances_ref, send_ref, held, rest, sems):
    load_weights(flags, (w0, w1, w2, w3, w4, w5, w6, w7), held, rest, sems)
    length, d = h_ref.shape
    h = h_ref[...]
    s = lax.rsqrt(jnp.mean(h * h, axis=-1, keepdims=True) + EPS)
    normed = (h * s * gm_ref[...]).astype(BF16)
    packed_ref[...] = dot(normed, held[...]).astype(BF16)
    size = d // heads
    scale = size ** (-0.5)
    same = mcol[...] == mrow[...]
    low = lax.broadcasted_iota(jnp.int32, (length, 2 * size), 1) < size
    for pair in range(heads // 2):
        at = slice(2 * size * pair, 2 * size * (pair + 1))
        q2 = packed_ref[:, at]
        k2 = packed_ref[:, d + at.start : d + at.stop]
        v2 = packed_ref[:, 2 * d + at.start : 2 * d + at.stop]
        zero = jnp.zeros_like(q2)
        pa = probs_of(jnp.where(low, q2, zero), k2, scale, bias_of(along_ref, 2 * pair, length), same)
        pb = probs_of(jnp.where(low, zero, q2), k2, scale, bias_of(along_ref, 2 * pair + 1, length), same)
        mixed_ref[:, at] = jnp.where(low, dot(pa.astype(BF16), v2), dot(pb.astype(BF16), v2)).astype(BF16)
    middle = h + dot(mixed_ref[...], rest[:, :d])
    middle_ref[...] = middle
    r = lax.rsqrt(jnp.mean(middle * middle, axis=-1, keepdims=True) + EPS)
    second = (middle * r * ge_ref[...]).astype(BF16)
    second_ref[...] = second
    logits = dot(second, rest[:, d:])
    lanes = lax.broadcasted_iota(jnp.int32, logits.shape, 1)
    logits = jnp.where(lanes < experts, logits, NEG)
    raised = jnp.exp(logits - jnp.max(logits, axis=-1, keepdims=True))
    chances_ref[...] = raised / jnp.sum(raised, axis=-1, keepdims=True)
    slots = send_ref.shape[0]
    hot = (lax.broadcasted_iota(jnp.int32, (slots, length), 0) == srow[...]).astype(F32).astype(BF16)
    send_ref[...] = dot(hot, second).astype(BF16)


def mixer_bwd(heads, flags, g_ref, h_ref, middle_ref, second_ref, packed_ref, mixed_ref, gm_ref, ge_ref,
              along_ref, mcol, mrow, scol, dlog_ref, ret_ref, w0, w1, w2, w3, w4, w5, w6, w7,
              dh_ref, grad_ref, tail_ref, gains_ref, diag_ref, held, rest, dpacked, sems):
    load_weights(flags, (w0, w1, w2, w3, w4, w5, w6, w7), held, rest, sems)
    length, d = h_ref.shape
    slots = ret_ref.shape[0]
    g = g_ref[...]
    dlog = dlog_ref[...]
    second = second_ref[...]
    hot = (lax.broadcasted_iota(jnp.int32, (length, slots), 1) == scol[...]).astype(F32).astype(BF16)
    dsecond = dot_nt(dlog, rest[:, d:]) + dot(hot, ret_ref[...])
    tail_ref[...] = dot_tn(second, dlog)
    middle = middle_ref[...]
    r = lax.rsqrt(jnp.mean(middle * middle, axis=-1, keepdims=True) + EPS)
    t = dsecond * ge_ref[...]
    dge = jnp.sum(dsecond * middle * r, axis=0, keepdims=True)
    dmiddle = g + r * t - middle * (r * r * r) * jnp.mean(middle * t, axis=-1, keepdims=True)
    dbranch = dmiddle.astype(BF16)
    grad_ref[:, 3 * d :] = dot_tn(mixed_ref[...], dbranch).astype(BF16)
    dmixed = dot_nt(dbranch, rest[:, :d]).astype(BF16)
    size = d // heads
    scale = size ** (-0.5)
    same = mcol[...] == mrow[...]
    low = lax.broadcasted_iota(jnp.int32, (length, 2 * size), 1) < size
    for pair in range(heads // 2):
        at = slice(2 * size * pair, 2 * size * (pair + 1))
        q2 = packed_ref[:, at]
        k2 = packed_ref[:, d + at.start : d + at.stop]
        v2 = packed_ref[:, 2 * d + at.start : 2 * d + at.stop]
        dm2 = dmixed[:, at]
        zero = jnp.zeros_like(q2)
        parts = []
        for which in range(2):
            mine = low if which == 0 else jnp.logical_not(low)
            head = 2 * pair + which
            p = probs_of(jnp.where(mine, q2, zero), k2, scale, bias_of(along_ref, head, length), same)
            dp = dot_nt(jnp.where(mine, dm2, zero), v2)
            ds = (p * (dp - jnp.sum(dp * p, axis=-1, keepdims=True))).astype(BF16)
            parts.append((dot(ds, k2), dot_tn(ds, q2), dot_tn(p.astype(BF16), dm2)))
            diag_ref[head] = ds
        dpacked[:, at] = (jnp.where(low, parts[0][0], parts[1][0]) * scale).astype(BF16)
        dpacked[:, d + at.start : d + at.stop] = (jnp.where(low, parts[0][1], parts[1][1]) * scale).astype(BF16)
        dpacked[:, 2 * d + at.start : 2 * d + at.stop] = jnp.where(low, parts[0][2], parts[1][2]).astype(BF16)
    h = h_ref[...]
    s = lax.rsqrt(jnp.mean(h * h, axis=-1, keepdims=True) + EPS)
    normed = (h * s * gm_ref[...]).astype(BF16)
    grad_ref[:, : 3 * d] = dot_tn(normed, dpacked[...]).astype(BF16)
    dnormed = dot_nt(dpacked[...], held[...])
    u = dnormed * gm_ref[...]
    dgm = jnp.sum(dnormed * h * s, axis=0, keepdims=True)
    dh_ref[...] = dmiddle + s * u - h * (s * s * s) * jnp.mean(h * u, axis=-1, keepdims=True)
    gains_ref[0:1, :] = dgm
    gains_ref[1:2, :] = dge


def ffn_fwd(flags, rows_ref, wi_own, wo_own, wi_oth, wo_oth, out_ref, acc):
    step = pl.program_id(0)

    @pl.when(step == 0)
    def _():
        acc[...] = jnp.zeros_like(acc)

    def work(wi, wo):
        hidden = gelu_parts(dot_nt(rows_ref[...], wi[...]))[0].astype(BF16)
        acc[...] += dot(hidden, wo[...])

    @pl.when(flags[0] == 1)
    def _():
        work(wi_own, wo_own)

    @pl.when(flags[0] == 0)
    def _():
        work(wi_oth, wo_oth)

    @pl.when(step == pl.num_programs(0) - 1)
    def _():
        out_ref[...] = acc[...].astype(BF16)


def ffn_bwd(flags, rows_ref, pull_ref, wi_own, wo_own, wi_oth, wo_oth, out_ref, acc):
    step = pl.program_id(0)

    @pl.when(step == 0)
    def _():
        acc[...] = jnp.zeros_like(acc)

    def work(wi, wo):
        before = dot_nt(rows_ref[...], wi[...])
        th = gelu_parts(before)[1]
        slope = (gelu_slope(before, th) * dot_nt(pull_ref[...], wo[...])).astype(BF16)
        acc[...] += dot(slope, wi[...])

    @pl.when(flags[0] == 1)
    def _():
        work(wi_own, wo_own)

    @pl.when(flags[0] == 0)
    def _():
        work(wi_oth, wo_oth)

    @pl.when(step == pl.num_programs(0) - 1)
    def _():
        out_ref[...] = acc[...].astype(BF16)


def weight_grads(flags, rows_ref, pull_ref, wi, wo, gin_ref, gout_ref):
    rows = rows_ref[...]
    pulls = pull_ref[...]
    before = dot_nt(rows, wi[...])
    act, th = gelu_parts(before)
    slope = (gelu_slope(before, th) * dot_nt(pulls, wo[...])).astype(BF16)
    gout_ref[...] = dot_tn(act.astype(BF16), pulls)
    gin_ref[...] = dot_tn(slope, rows)


def call_ffn(kernel, flags, arrays, own, oth):
    rows, d = arrays[0].shape
    f = own[0].shape[0]
    block = 512 if f % 512 == 0 else f
    whole = pl.BlockSpec((rows, d), lambda i, s: (0, 0))
    mine = pl.BlockSpec((block, d), lambda i, s: (i * s[0], 0))
    theirs = pl.BlockSpec((block, d), lambda i, s: (i * (1 - s[0]), 0))
    n = len(arrays)
    return pl.pallas_call(
        kernel,
        out_shape=jax.ShapeDtypeStruct((rows, d), BF16),
        grid_spec=pltpu.PrefetchScalarGridSpec(
            num_scalar_prefetch=1,
            grid=(f // block,),
            in_specs=[whole] * n + [mine, mine, theirs, theirs],
            out_specs=whole,
            scratch_shapes=[pltpu.VMEM((rows, d), F32)],
        ),
        compiler_params=pltpu.CompilerParams(vmem_limit_bytes=VMEM),
        cost_estimate=pl.CostEstimate(
            flops=4 * n * rows * d * f, bytes_accessed=4 * f * d + 4 * rows * d, transcendentals=rows * f
        ),
    )(flags, *arrays, *own, *oth)


def call_grads(flags, rows, pulls, wi, wo):
    count, d = rows.shape
    f = wi.shape[0] // 2
    block = 256
    steps = f // block
    whole = pl.BlockSpec((count, d), lambda i, s: (0, 0))
    part = pl.BlockSpec((block, d), lambda i, s: (s[1] * steps + i, 0))
    out = pl.BlockSpec((block, d), lambda i, s: (i, 0))
    return pl.pallas_call(
        weight_grads,
        out_shape=[jax.ShapeDtypeStruct((f, d), F32)] * 2,
        grid_spec=pltpu.PrefetchScalarGridSpec(
            num_scalar_prefetch=1,
            grid=(steps,),
            in_specs=[whole, whole, part, part],
            out_specs=[out, out],
        ),
        compiler_params=pltpu.CompilerParams(vmem_limit_bytes=VMEM),
        cost_estimate=pl.CostEstimate(
            flops=8 * count * d * f, bytes_accessed=12 * f * d, transcendentals=count * f
        ),
    )(flags, rows, pulls, wi, wo)


def call_mixer(kernel, flags, arrays, weights, outs, extra):
    vm = pl.BlockSpec(memory_space=pltpu.VMEM)
    half, cols = weights[0].shape
    return pl.pallas_call(
        kernel,
        out_shape=[jax.ShapeDtypeStruct(shape, kind) for shape, kind in outs],
        in_specs=[pl.BlockSpec(memory_space=pltpu.SMEM)]
        + [vm] * len(arrays)
        + [pl.BlockSpec(memory_space=pl.ANY)] * 8,
        out_specs=[vm] * len(outs),
        scratch_shapes=[pltpu.VMEM((2 * half, cols), BF16), pltpu.VMEM((2 * half, weights[4].shape[1]), BF16)]
        + extra
        + [pltpu.SemaphoreType.DMA((4,))],
        compiler_params=pltpu.CompilerParams(vmem_limit_bytes=VMEM),
        cost_estimate=pl.CostEstimate(
            flops=3 * 10**9, bytes_accessed=10**7, transcendentals=10**5
        ),
    )(flags, *arrays, *weights)


def swap(x, axis):
    return lax.ppermute(x, axis, [(0, 1), (1, 0)])


def only(x, axis, layer, by):
    n = lax.axis_size(axis)
    return lax.ppermute(x, ("section", axis), [(layer * n + i, layer * n + (i ^ by)) for i in range(n)])


def across(x, layer):
    return lax.ppermute(x, "section", [(1 - layer, layer)])


def after(x, y):
    return lax.optimization_barrier((x, y))[0]


def begin_sum(grad, tail):
    c = lax.axis_index("section")
    cols = grad.shape[1] // 2
    tail = tail.astype(BF16)
    keep = jnp.concatenate([lax.dynamic_slice_in_dim(grad, c * cols, cols, 1), tail], axis=1)
    send = jnp.concatenate([lax.dynamic_slice_in_dim(grad, (1 - c) * cols, cols, 1), tail], axis=1)
    return keep, swap(send, "section")


def added(pair, kind=BF16):
    return (pair[0].astype(F32) + pair[1].astype(F32)).astype(kind)


def halve(part, step):
    c, e, y = lax.axis_index("section"), lax.axis_index("expert"), lax.axis_index("shard")
    n = lax.axis_size("expert")
    cols = part.shape[1]
    x = e % 2
    if step < 2:
        pairs = []
        for i in range(2 * n * 2):
            along_y = (i // (2 * n)) == step
            pairs.append((i, i ^ (1 if along_y else 2)))
        got_axes = ("section", "expert", "shard")
        by_y = c == step
        if step == 0:
            view = part.reshape(n // 2, 4, -1, cols)
            firsts = (jnp.where(by_y, y, 2 * x), jnp.where(by_y, 2 + y, 2 * x + 1))
            others = (jnp.where(by_y, 1 - y, 2 - 2 * x), jnp.where(by_y, 3 - y, 3 - 2 * x))
            keep, send = (
                jnp.stack([lax.dynamic_index_in_dim(view, i, 1, keepdims=False) for i in both], axis=1)
                for both in (firsts, others)
            )
        else:
            view = part.reshape(n // 2, 2, -1, cols)
            bit = jnp.where(by_y, y, x)
            keep = lax.dynamic_index_in_dim(view, bit, 1, keepdims=False)
            send = lax.dynamic_index_in_dim(view, 1 - bit, 1, keepdims=False)
        keep, send = keep.reshape(-1, cols), send.reshape(-1, cols)
        return keep, lax.ppermute(send, got_axes, pairs)
    by = 1 << (step - 1)
    bit = (e // by) % 2
    view = part.reshape(n // (2 * by), 2, -1, cols)
    keep = lax.dynamic_index_in_dim(view, bit, 1, keepdims=False).reshape(-1, cols)
    send = lax.dynamic_index_in_dim(view, 1 - bit, 1, keepdims=False).reshape(-1, cols)
    return keep, lax.ppermute(send, "expert", [(i, i ^ by) for i in range(n)])


def exchange(x, n):
    slots, d = x.shape
    return lax.all_to_all(
        x.reshape(n, slots // n, d), "expert", split_axis=0, concat_axis=0, tiled=True
    ).reshape(slots, d)


def shards(
    stream, segments, routes, room, project_in, project_out, bias_table, gain_mixer, gain_expert,
    router, expert_in, expert_out, cotangent,
):
    c = lax.axis_index("section")
    y = lax.axis_index("shard")
    n = lax.axis_size("expert")
    length, d = stream.shape[1:]
    heads = bias_table.shape[2]
    labels_n = bias_table.shape[1]
    experts = router.shape[2]
    capacity = max(2, 3 * length // (2 * experts))
    slots_all = experts * capacity
    table_size = labels_n * heads

    first = project_in[0]
    other = jnp.concatenate([project_out[0], jnp.pad(router[0], ((0, 0), (0, 128 - experts)))], axis=1)
    first_peer0 = only(first, "shard", 0, 1)
    other_peer0 = only(after(other, first_peer0), "shard", 0, 1)
    wi, wo = expert_in[0, 0], expert_out[0, 0]
    small = jnp.concatenate(
        [bias_table[0].reshape(-1), gain_mixer[0], gain_expert[0], room[0].astype(F32)]
    )
    small_other = swap(small, "section")
    route_here = lax.dynamic_index_in_dim(routes[0], c, 0, keepdims=False)[0]
    route_other = swap(lax.dynamic_index_in_dim(routes[0], 1 - c, 0, keepdims=False)[0], "section")
    first_over0 = (across(first, 1), across(first_peer0, 1))
    other_over0 = (across(other, 1), across(other_peer0, 1))
    wi_other = swap(wi, "section")
    wo_other = swap(after(wo, first_peer0), "section")
    first1, other1 = after((first, other), other_peer0)
    first_peer1, other_peer1 = only(first1, "shard", 1, 1), only(other1, "shard", 1, 1)
    weights = (
        (first, first_peer0, *first_over0, other, other_peer0, *other_over0),
        (first, first_peer1, across(first1, 0), across(first_peer1, 0),
         other, other_peer1, across(other1, 0), across(other_peer1, 0)),
    )
    marks = lax.dynamic_index_in_dim(segments, c, 0, keepdims=False)
    mcol, mrow = marks.reshape(length, 1), marks.reshape(1, length)
    offsets = jnp.arange(2 * length, dtype=jnp.int32) - (length - 1)
    hits = (buckets(offsets)[:, None] == jnp.arange(labels_n, dtype=jnp.int32)[None, :]).astype(F32)

    given = []
    for layer in range(2):
        mine = c == layer
        flags = jnp.stack([mine.astype(jnp.int32), y.astype(jnp.int32)])
        values = jnp.where(mine, small, small_other)
        table = values[:table_size].reshape(labels_n, heads)
        gm = values[table_size : table_size + d].reshape(1, d)
        ge = values[table_size + d : table_size + 2 * d].reshape(1, d)
        limits = values[table_size + 2 * d :].astype(jnp.int32)
        chosen = jnp.where(mine, route_here, route_other)
        along = jnp.dot(table.T, hits.T, precision=HIGHEST)
        picks = chosen[:, None] == jnp.arange(experts, dtype=jnp.int32)[None, :]
        earlier = jnp.tril(jnp.ones((length, length), BF16), -1)
        counts = dot(earlier, picks.astype(BF16)).astype(jnp.int32)
        rank = jnp.sum(jnp.where(picks, counts, 0), axis=-1)
        limit = jnp.sum(jnp.where(picks, limits[None, :], 0), axis=-1)
        slots = jnp.where(rank < limit, chosen * capacity + rank, slots_all)
        given.append((flags, gm, ge, along, chosen, slots))

    current = lax.dynamic_index_in_dim(stream, c, 0, keepdims=False).astype(F32)
    saved = []
    for layer in range(2):
        flags, gm, ge, along, chosen, slots = given[layer]
        scol, srow = slots.reshape(length, 1), slots.reshape(1, length)
        packed, mixed, middle, second, chances, sending = call_mixer(
            functools.partial(mixer_fwd, heads, experts),
            flags,
            (current, gm, ge, along, mcol, mrow, srow),
            weights[layer],
            [
                ((length, 3 * d), BF16),
                ((length, d), BF16),
                ((length, d), F32),
                ((length, d), BF16),
                ((length, 128), F32),
                ((slots_all, d), BF16),
            ],
            [],
        )
        rows = exchange(sending, n)
        output = call_ffn(ffn_fwd, flags, (rows,), (wi, wo), (wi_other, wo_other))
        back = exchange(output, n)
        hot = (jnp.arange(slots_all, dtype=jnp.int32)[None, :] == scol).astype(BF16)
        picked = dot(hot, back)
        lane = jnp.arange(128, dtype=jnp.int32)[None, :] == chosen[:, None]
        gate = jnp.sum(jnp.where(lane, chances, 0.0), axis=-1, keepdims=True)
        result = middle + gate * picked
        saved.append((current, packed, mixed, middle, second, chances, rows, picked, gate, lane))
        current = result.astype(BF16).astype(F32)
    final = result

    rows_mine = jnp.where(c == 0, saved[0][6], saved[1][6])
    rows_sent = swap(jnp.where(c == 0, saved[1][6], saved[0][6]), "section")
    rows_pair = jnp.concatenate([rows_mine, rows_sent], axis=0)
    rows_all = jnp.concatenate([rows_pair, swap(rows_pair, "shard")], axis=0)

    pull = lax.dynamic_index_in_dim(cotangent, c, 0, keepdims=False).astype(F32)
    pulls = [None, None]
    reduced = [None, None]
    rounds = n.bit_length()
    step, pair = 0, None
    for layer in (1, 0):
        flags, gm, ge, along, chosen, slots = given[layer]
        inputs, packed, mixed, middle, second, chances, rows, picked, gate, lane = saved[layer]
        scol, srow = slots.reshape(length, 1), slots.reshape(1, length)
        pull_gate = jnp.sum(pull * picked, axis=-1, keepdims=True)
        pull_logits = (chances * (jnp.where(lane, pull_gate, 0.0) - pull_gate * gate)).astype(BF16)
        pull_picked = (gate * pull).astype(BF16)
        hot = (jnp.arange(slots_all, dtype=jnp.int32)[:, None] == srow).astype(BF16)
        sending = dot(hot, pull_picked).astype(BF16)
        if layer == 0:
            part, sending = lax.optimization_barrier((added(pair), sending))
            pair = halve(part, 0)
        pulls[layer] = exchange(sending, n)
        back_rows = call_ffn(ffn_bwd, flags, (rows, pulls[layer]), (wi, wo), (wi_other, wo_other))
        if layer == 0:
            part, back_rows = lax.optimization_barrier((added(pair), back_rows))
            pair = halve(part, 1)
        returned = exchange(back_rows, n)
        if layer == 0:
            part, returned = lax.optimization_barrier((added(pair), returned))
            pair = halve(part, 2)
        d_inputs, grad, tail, gains, grid = call_mixer(
            functools.partial(mixer_bwd, heads),
            flags,
            (pull, inputs, middle, second, packed, mixed, gm, ge, along, mcol, mrow, scol, pull_logits, returned),
            weights[layer],
            [
                ((length, d), F32),
                ((d, 4 * d), BF16),
                ((d, 128), F32),
                ((8, d), F32),
                ((heads, length, length), BF16),
            ],
            [pltpu.VMEM((length, 3 * d), BF16)],
        )
        places = jnp.arange(length, dtype=jnp.int32)
        which = buckets(places[None, :] - places[:, None])
        each = (which[None] == jnp.arange(labels_n, dtype=jnp.int32)[:, None, None]).astype(BF16)
        grad_table = jnp.einsum("bij,hij->bh", each, grid, preferred_element_type=F32)
        devices = 2 * n
        padded = jnp.pad(
            grad_table.reshape(devices, -1), ((0, 0), (0, d // devices - table_size // devices))
        ) if d // devices >= table_size // devices else None
        smalls = jnp.stack([gains[0], gains[1], padded.reshape(d)], axis=1)
        tail = jnp.concatenate([tail[:, :experts], smalls, jnp.zeros((d, 125 - experts), F32)], axis=1)
        if layer == 1:
            pair = begin_sum(grad, tail)
        else:
            for step in range(3, rounds):
                pair = halve(added(pair), step)
            reduced[1] = added(pair, F32)
            pair = begin_sum(grad, tail)
            for step in range(rounds):
                pair = halve(added(pair), step)
            reduced[0] = added(pair, F32)
        pull = d_inputs.astype(BF16).astype(F32)

    pull_mine = jnp.where(c == 0, pulls[0], pulls[1])
    pull_sent = swap(jnp.where(c == 0, pulls[1], pulls[0]), "section")
    pull_pair = jnp.concatenate([pull_mine, pull_sent], axis=0)
    pull_all = jnp.concatenate([pull_pair, swap(pull_pair, "shard")], axis=0)
    grad_in, grad_out = call_grads(given[0][0], rows_all, pull_all, wi, wo)

    got = swap(jnp.where(c == 0, final, d_inputs), "section")
    ends = jnp.stack([jnp.where(c == 0, d_inputs, got), jnp.where(c == 0, got, final)])
    here = jnp.where(c == 0, reduced[0], reduced[1])
    there = swap(jnp.where(c == 0, reduced[1], reduced[0])[:, : 2 * d], "section")
    body = here[:, : 2 * d]
    total = jnp.concatenate(
        [jnp.where(c == 0, body, there), jnp.where(c == 0, there, body), here[:, 2 * d :]], axis=1
    )
    at = 4 * d + experts
    share = table_size // (2 * n)
    return (
        ends[None],
        total[None, :, : 3 * d],
        total[None, :, 3 * d : 4 * d],
        total[None, :share, at + 2],
        total[None, :, at],
        total[None, :, at + 1],
        total[None, :, 4 * d : at],
        grad_in[None, None],
        grad_out[None, None],
    )


def solution(mesh):
    placed = (
        P(None, ("expert", "shard"), None),
        P(None, ("expert", "shard"), None),
        P("section", None, ("expert", "shard"), None),
        P("section", None),
        P("section", "shard", None),
        P("section", "shard", None),
        P("section", None, None),
        P("section", None),
        P("section", None),
        P("section", "shard", None),
        P("section", "expert", None, None),
        P("section", "expert", None, None),
        P(None, ("expert", "shard"), None),
    )
    return jax.shard_map(
        shards,
        mesh=mesh,
        in_specs=placed,
        out_specs=(
            P("section", None, ("expert", "shard"), None),
            P("section", ("expert", "shard"), None),
            P("section", ("expert", "shard"), None),
            P("section", ("expert", "shard")),
            P("section", ("expert", "shard")),
            P("section", ("expert", "shard")),
            P("section", ("expert", "shard"), None),
            P("section", "expert", "shard", None),
            P("section", "expert", "shard", None),
        ),
        check_vma=False,
    )
```

```python
import functools

import jax
import jax.numpy as jnp
from jax import lax
from jax.experimental import pallas as pl
from jax.experimental.pallas import tpu as pltpu
from jax.sharding import PartitionSpec as P

EPS = 1e-06
NEG = -1e30
SPLITS = (12, 16, 23, 32, 46, 64, 91)
HIGHEST = lax.Precision.HIGHEST
F32 = jnp.float32
BF16 = jnp.bfloat16
GELU_A = 0.7978845608028654
GELU_B = 0.044715
VMEM = 48 * 1024 * 1024


def dot(a, b):
    return lax.dot_general(a, b, (((1,), (0,)), ((), ())), preferred_element_type=F32)


def dot_nt(a, b):
    return lax.dot_general(a, b, (((1,), (1,)), ((), ())), preferred_element_type=F32)


def dot_tn(a, b):
    return lax.dot_general(a, b, (((0,), (0,)), ((), ())), preferred_element_type=F32)


def column_sum(values, pick):
    return lax.dot_general(
        values, pick, (((0,), (0,)), ((), ())), precision=HIGHEST, preferred_element_type=F32
    )


def gelu_parts(v):
    th = jnp.tanh(GELU_A * (v + GELU_B * v * v * v))
    return 0.5 * v * (1.0 + th), th


def gelu_slope(v, th):
    return 0.5 * (1.0 + th) + 0.5 * v * (1.0 - th * th) * (GELU_A * (1.0 + 3.0 * GELU_B * v * v))


def buckets(offset):
    span = jnp.abs(offset)
    far = 8 + sum(((span >= limit).astype(jnp.int32) for limit in SPLITS))
    return jnp.where(span < 8, span, far) + 16 * (offset > 0).astype(jnp.int32)


def load_weights(flags, refs, held, rest, sems):
    half = refs[0].shape[0]
    y = flags[1]
    low = pl.ds(pl.multiple_of(y * half, half), half)
    high = pl.ds(pl.multiple_of((1 - y) * half, half), half)

    def all_four(sources):
        places = (held.at[low], held.at[high], rest.at[low], rest.at[high])
        copies = [pltpu.make_async_copy(a, b, sems.at[i]) for i, (a, b) in enumerate(zip(sources, places))]
        for copy in copies:
            copy.start()
        for copy in copies:
            copy.wait()

    @pl.when(flags[0] == 1)
    def _():
        all_four((refs[0], refs[1], refs[4], refs[5]))

    @pl.when(flags[0] == 0)
    def _():
        all_four((refs[2], refs[3], refs[6], refs[7]))


def bias_of(along, head, length):
    wide = jnp.broadcast_to(along[head : head + 1, :], (length, 2 * length))
    return pltpu.roll(wide, length + 1, 1, stride=1, stride_axis=0)[:, :length]


def probs_of(q, k2, scale, bias, same):
    scores = dot_nt(q, k2) * scale + bias
    scores = jnp.where(same, scores, NEG)
    peak = jnp.max(scores, axis=-1, keepdims=True)
    raised = jnp.exp(scores - peak)
    return raised / jnp.sum(raised, axis=-1, keepdims=True)


def mixer_fwd(heads, experts, flags, h_ref, gm_ref, ge_ref, along_ref, mcol, mrow, srow, w0, w1, w2, w3,
              w4, w5, w6, w7, packed_ref, mixed_ref, middle_ref, second_ref, chances_ref, send_ref, held, rest, sems):
    load_weights(flags, (w0, w1, w2, w3, w4, w5, w6, w7), held, rest, sems)
    length, d = h_ref.shape
    h = h_ref[...]
    s = lax.rsqrt(jnp.mean(h * h, axis=-1, keepdims=True) + EPS)
    normed = (h * s * gm_ref[...]).astype(BF16)
    packed_ref[...] = dot(normed, held[...]).astype(BF16)
    size = d // heads
    scale = size ** (-0.5)
    same = mcol[...] == mrow[...]
    low = lax.broadcasted_iota(jnp.int32, (length, 2 * size), 1) < size
    for pair in range(heads // 2):
        at = slice(2 * size * pair, 2 * size * (pair + 1))
        q2 = packed_ref[:, at]
        k2 = packed_ref[:, d + at.start : d + at.stop]
        v2 = packed_ref[:, 2 * d + at.start : 2 * d + at.stop]
        zero = jnp.zeros_like(q2)
        pa = probs_of(jnp.where(low, q2, zero), k2, scale, bias_of(along_ref, 2 * pair, length), same)
        pb = probs_of(jnp.where(low, zero, q2), k2, scale, bias_of(along_ref, 2 * pair + 1, length), same)
        mixed_ref[:, at] = jnp.where(low, dot(pa.astype(BF16), v2), dot(pb.astype(BF16), v2)).astype(BF16)
    middle = h + dot(mixed_ref[...], rest[:, :d])
    middle_ref[...] = middle
    r = lax.rsqrt(jnp.mean(middle * middle, axis=-1, keepdims=True) + EPS)
    second = (middle * r * ge_ref[...]).astype(BF16)
    second_ref[...] = second
    logits = dot(second, rest[:, d:])
    lanes = lax.broadcasted_iota(jnp.int32, logits.shape, 1)
    logits = jnp.where(lanes < experts, logits, NEG)
    raised = jnp.exp(logits - jnp.max(logits, axis=-1, keepdims=True))
    chances_ref[...] = raised / jnp.sum(raised, axis=-1, keepdims=True)
    slots = send_ref.shape[0]
    hot = (lax.broadcasted_iota(jnp.int32, (slots, length), 0) == srow[...]).astype(F32).astype(BF16)
    send_ref[...] = dot(hot, second).astype(BF16)


def mixer_bwd(heads, experts, flags, g_ref, h_ref, middle_ref, second_ref, packed_ref, mixed_ref, gm_ref, ge_ref,
              along_ref, mcol, mrow, scol, dlog_ref, ret_ref, w0, w1, w2, w3, w4, w5, w6, w7,
              dh_ref, keep_ref, send_ref, diag_ref, held, rest, dpacked, sems):
    load_weights(flags, (w0, w1, w2, w3, w4, w5, w6, w7), held, rest, sems)
    length, d = h_ref.shape
    slots = ret_ref.shape[0]
    g = g_ref[...]
    dlog = dlog_ref[...]
    second = second_ref[...]
    hot = (lax.broadcasted_iota(jnp.int32, (length, slots), 1) == scol[...]).astype(F32).astype(BF16)
    dsecond = dot_nt(dlog, rest[:, d:]) + dot(hot, ret_ref[...])
    tail = dot_tn(second, dlog)
    middle = middle_ref[...]
    r = lax.rsqrt(jnp.mean(middle * middle, axis=-1, keepdims=True) + EPS)
    t = dsecond * ge_ref[...]
    ones = lax.broadcasted_iota(jnp.int32, (length, 128), 1)
    tail += column_sum(dsecond * middle * r, (ones == experts + 1).astype(F32))
    dmiddle = g + r * t - middle * (r * r * r) * jnp.mean(middle * t, axis=-1, keepdims=True)
    dbranch = dmiddle.astype(BF16)
    grad_out = dot_tn(mixed_ref[...], dbranch).astype(BF16)
    dmixed = dot_nt(dbranch, rest[:, :d]).astype(BF16)
    size = d // heads
    scale = size ** (-0.5)
    same = mcol[...] == mrow[...]
    low = lax.broadcasted_iota(jnp.int32, (length, 2 * size), 1) < size
    for pair in range(heads // 2):
        at = slice(2 * size * pair, 2 * size * (pair + 1))
        q2 = packed_ref[:, at]
        k2 = packed_ref[:, d + at.start : d + at.stop]
        v2 = packed_ref[:, 2 * d + at.start : 2 * d + at.stop]
        dm2 = dmixed[:, at]
        zero = jnp.zeros_like(q2)
        parts = []
        for which in range(2):
            mine = low if which == 0 else jnp.logical_not(low)
            head = 2 * pair + which
            p = probs_of(jnp.where(mine, q2, zero), k2, scale, bias_of(along_ref, head, length), same)
            dp = dot_nt(jnp.where(mine, dm2, zero), v2)
            ds = (p * (dp - jnp.sum(dp * p, axis=-1, keepdims=True))).astype(BF16)
            parts.append((dot(ds, k2), dot_tn(ds, q2), dot_tn(p.astype(BF16), dm2)))
            diag_ref[head] = ds
        dpacked[:, at] = (jnp.where(low, parts[0][0], parts[1][0]) * scale).astype(BF16)
        dpacked[:, d + at.start : d + at.stop] = (jnp.where(low, parts[0][1], parts[1][1]) * scale).astype(BF16)
        dpacked[:, 2 * d + at.start : 2 * d + at.stop] = jnp.where(low, parts[0][2], parts[1][2]).astype(BF16)
    h = h_ref[...]
    s = lax.rsqrt(jnp.mean(h * h, axis=-1, keepdims=True) + EPS)
    normed = (h * s * gm_ref[...]).astype(BF16)
    dnormed = dot_nt(dpacked[...], held[...])
    u = dnormed * gm_ref[...]
    tail += column_sum(dnormed * h * s, (ones == experts).astype(F32))
    dh_ref[...] = dmiddle + s * u - h * (s * s * s) * jnp.mean(h * u, axis=-1, keepdims=True)
    tail = tail.astype(BF16)
    keep_ref[:, 2 * d :] = tail
    send_ref[:, 2 * d :] = tail

    def halves(low_ref, high_ref):
        low_ref[:, : 2 * d] = dot_tn(normed, dpacked[:, : 2 * d]).astype(BF16)
        high_ref[:, :d] = dot_tn(normed, dpacked[:, 2 * d :]).astype(BF16)
        high_ref[:, d : 2 * d] = grad_out

    @pl.when(flags[2] == 0)
    def _():
        halves(keep_ref, send_ref)

    @pl.when(flags[2] == 1)
    def _():
        halves(send_ref, keep_ref)


def ffn_fwd(flags, rows_ref, wi_own, wo_own, wi_oth, wo_oth, out_ref, acc):
    step = pl.program_id(0)

    @pl.when(step == 0)
    def _():
        acc[...] = jnp.zeros_like(acc)

    def work(wi, wo):
        hidden = gelu_parts(dot_nt(rows_ref[...], wi[...]))[0].astype(BF16)
        acc[...] += dot(hidden, wo[...])

    @pl.when(flags[0] == 1)
    def _():
        work(wi_own, wo_own)

    @pl.when(flags[0] == 0)
    def _():
        work(wi_oth, wo_oth)

    @pl.when(step == pl.num_programs(0) - 1)
    def _():
        out_ref[...] = acc[...].astype(BF16)


def ffn_bwd(flags, rows_ref, pull_ref, wi_own, wo_own, wi_oth, wo_oth, out_ref, acc):
    step = pl.program_id(0)

    @pl.when(step == 0)
    def _():
        acc[...] = jnp.zeros_like(acc)

    def work(wi, wo):
        before = dot_nt(rows_ref[...], wi[...])
        th = gelu_parts(before)[1]
        slope = (gelu_slope(before, th) * dot_nt(pull_ref[...], wo[...])).astype(BF16)
        acc[...] += dot(slope, wi[...])

    @pl.when(flags[0] == 1)
    def _():
        work(wi_own, wo_own)

    @pl.when(flags[0] == 0)
    def _():
        work(wi_oth, wo_oth)

    @pl.when(step == pl.num_programs(0) - 1)
    def _():
        out_ref[...] = acc[...].astype(BF16)


def weight_grads(flags, rows_ref, pull_ref, wi, wo, gin_ref, gout_ref):
    rows = rows_ref[...]
    pulls = pull_ref[...]
    before = dot_nt(rows, wi[...])
    act, th = gelu_parts(before)
    slope = (gelu_slope(before, th) * dot_nt(pulls, wo[...])).astype(BF16)
    gout_ref[...] = dot_tn(act.astype(BF16), pulls)
    gin_ref[...] = dot_tn(slope, rows)


def call_ffn(kernel, flags, arrays, own, oth):
    rows, d = arrays[0].shape
    f = own[0].shape[0]
    block = 512 if f % 512 == 0 else f
    whole = pl.BlockSpec((rows, d), lambda i, s: (0, 0))
    mine = pl.BlockSpec((block, d), lambda i, s: (i * s[0], 0))
    theirs = pl.BlockSpec((block, d), lambda i, s: (i * (1 - s[0]), 0))
    n = len(arrays)
    return pl.pallas_call(
        kernel,
        out_shape=jax.ShapeDtypeStruct((rows, d), BF16),
        grid_spec=pltpu.PrefetchScalarGridSpec(
            num_scalar_prefetch=1,
            grid=(f // block,),
            in_specs=[whole] * n + [mine, mine, theirs, theirs],
            out_specs=whole,
            scratch_shapes=[pltpu.VMEM((rows, d), F32)],
        ),
        compiler_params=pltpu.CompilerParams(vmem_limit_bytes=VMEM),
        cost_estimate=pl.CostEstimate(
            flops=4 * n * rows * d * f, bytes_accessed=4 * f * d + 4 * rows * d, transcendentals=rows * f
        ),
    )(flags, *arrays, *own, *oth)


def call_grads(flags, rows, pulls, wi, wo):
    count, d = rows.shape
    f = wi.shape[0] // 2
    block = 256
    steps = f // block
    whole = pl.BlockSpec((count, d), lambda i, s: (0, 0))
    part = pl.BlockSpec((block, d), lambda i, s: (s[1] * steps + i, 0))
    out = pl.BlockSpec((block, d), lambda i, s: (i, 0))
    return pl.pallas_call(
        weight_grads,
        out_shape=[jax.ShapeDtypeStruct((f, d), F32)] * 2,
        grid_spec=pltpu.PrefetchScalarGridSpec(
            num_scalar_prefetch=1,
            grid=(steps,),
            in_specs=[whole, whole, part, part],
            out_specs=[out, out],
        ),
        compiler_params=pltpu.CompilerParams(vmem_limit_bytes=VMEM),
        cost_estimate=pl.CostEstimate(
            flops=8 * count * d * f, bytes_accessed=12 * f * d, transcendentals=count * f
        ),
    )(flags, rows, pulls, wi, wo)


def call_mixer(kernel, flags, arrays, weights, outs, extra):
    vm = pl.BlockSpec(memory_space=pltpu.VMEM)
    half, cols = weights[0].shape
    return pl.pallas_call(
        kernel,
        out_shape=[jax.ShapeDtypeStruct(shape, kind) for shape, kind in outs],
        in_specs=[pl.BlockSpec(memory_space=pltpu.SMEM)]
        + [vm] * len(arrays)
        + [pl.BlockSpec(memory_space=pl.ANY)] * 8,
        out_specs=[vm] * len(outs),
        scratch_shapes=[pltpu.VMEM((2 * half, cols), BF16), pltpu.VMEM((2 * half, weights[4].shape[1]), BF16)]
        + extra
        + [pltpu.SemaphoreType.DMA((4,))],
        compiler_params=pltpu.CompilerParams(vmem_limit_bytes=VMEM),
        cost_estimate=pl.CostEstimate(
            flops=3 * 10**9, bytes_accessed=10**7, transcendentals=10**5
        ),
    )(flags, *arrays, *weights)


def swap(x, axis):
    return lax.ppermute(x, axis, [(0, 1), (1, 0)])


def only(x, axis, layer, by):
    n = lax.axis_size(axis)
    return lax.ppermute(x, ("section", axis), [(layer * n + i, layer * n + (i ^ by)) for i in range(n)])


def across(x, layer):
    return lax.ppermute(x, "section", [(1 - layer, layer)])


def after(x, y):
    return lax.optimization_barrier((x, y))[0]


def added(pair, kind=BF16):
    return (pair[0].astype(F32) + pair[1].astype(F32)).astype(kind)


def halve(part, step):
    c, e, y = lax.axis_index("section"), lax.axis_index("expert"), lax.axis_index("shard")
    n = lax.axis_size("expert")
    cols = part.shape[1]
    x = e % 2
    if step < 2:
        pairs = []
        for i in range(2 * n * 2):
            along_y = (i // (2 * n)) == step
            pairs.append((i, i ^ (1 if along_y else 2)))
        got_axes = ("section", "expert", "shard")
        by_y = c == step
        if step == 0:
            view = part.reshape(n // 2, 4, -1, cols)
            firsts = (jnp.where(by_y, y, 2 * x), jnp.where(by_y, 2 + y, 2 * x + 1))
            others = (jnp.where(by_y, 1 - y, 2 - 2 * x), jnp.where(by_y, 3 - y, 3 - 2 * x))
            keep, send = (
                jnp.stack([lax.dynamic_index_in_dim(view, i, 1, keepdims=False) for i in both], axis=1)
                for both in (firsts, others)
            )
        else:
            view = part.reshape(n // 2, 2, -1, cols)
            bit = jnp.where(by_y, y, x)
            keep = lax.dynamic_index_in_dim(view, bit, 1, keepdims=False)
            send = lax.dynamic_index_in_dim(view, 1 - bit, 1, keepdims=False)
        keep, send = keep.reshape(-1, cols), send.reshape(-1, cols)
        return keep, lax.ppermute(send, got_axes, pairs)
    by = 1 << (step - 1)
    bit = (e // by) % 2
    view = part.reshape(n // (2 * by), 2, -1, cols)
    keep = lax.dynamic_index_in_dim(view, bit, 1, keepdims=False).reshape(-1, cols)
    send = lax.dynamic_index_in_dim(view, 1 - bit, 1, keepdims=False).reshape(-1, cols)
    return keep, lax.ppermute(send, "expert", [(i, i ^ by) for i in range(n)])


def exchange(x, n):
    slots, d = x.shape
    return lax.all_to_all(
        x.reshape(n, slots // n, d), "expert", split_axis=0, concat_axis=0, tiled=True
    ).reshape(slots, d)


def shards(
    stream, segments, routes, room, project_in, project_out, bias_table, gain_mixer, gain_expert,
    router, expert_in, expert_out, cotangent,
):
    c = lax.axis_index("section")
    y = lax.axis_index("shard")
    n = lax.axis_size("expert")
    length, d = stream.shape[1:]
    heads = bias_table.shape[2]
    labels_n = bias_table.shape[1]
    experts = router.shape[2]
    capacity = max(2, 3 * length // (2 * experts))
    slots_all = experts * capacity
    table_size = labels_n * heads

    first = project_in[0]
    other = jnp.concatenate([project_out[0], jnp.pad(router[0], ((0, 0), (0, 128 - experts)))], axis=1)
    first_peer0 = only(first, "shard", 0, 1)
    other_peer0 = only(after(other, first_peer0), "shard", 0, 1)
    wi, wo = expert_in[0, 0], expert_out[0, 0]
    small = jnp.concatenate(
        [bias_table[0].reshape(-1), gain_mixer[0], gain_expert[0], room[0].astype(F32)]
    )
    small_other = swap(small, "section")
    route_here = lax.dynamic_index_in_dim(routes[0], c, 0, keepdims=False)[0]
    route_other = swap(lax.dynamic_index_in_dim(routes[0], 1 - c, 0, keepdims=False)[0], "section")
    first_over0 = (across(first, 1), across(first_peer0, 1))
    other_over0 = (across(other, 1), across(other_peer0, 1))
    wi_other = swap(wi, "section")
    wo_other = swap(after(wo, first_peer0), "section")
    first1, other1 = after((first, other), other_peer0)
    first_peer1, other_peer1 = only(first1, "shard", 1, 1), only(other1, "shard", 1, 1)
    weights = (
        (first, first_peer0, *first_over0, other, other_peer0, *other_over0),
        (first, first_peer1, across(first1, 0), across(first_peer1, 0),
         other, other_peer1, across(other1, 0), across(other_peer1, 0)),
    )
    marks = lax.dynamic_index_in_dim(segments, c, 0, keepdims=False)
    mcol, mrow = marks.reshape(length, 1), marks.reshape(1, length)
    offsets = jnp.arange(2 * length, dtype=jnp.int32) - (length - 1)
    hits = (buckets(offsets)[:, None] == jnp.arange(labels_n, dtype=jnp.int32)[None, :]).astype(F32)

    given = []
    for layer in range(2):
        mine = c == layer
        flags = jnp.stack([mine.astype(jnp.int32), y.astype(jnp.int32), c.astype(jnp.int32)])
        values = jnp.where(mine, small, small_other)
        table = values[:table_size].reshape(labels_n, heads)
        gm = values[table_size : table_size + d].reshape(1, d)
        ge = values[table_size + d : table_size + 2 * d].reshape(1, d)
        limits = values[table_size + 2 * d :].astype(jnp.int32)
        chosen = jnp.where(mine, route_here, route_other)
        along = jnp.dot(table.T, hits.T, precision=HIGHEST)
        picks = chosen[:, None] == jnp.arange(experts, dtype=jnp.int32)[None, :]
        earlier = jnp.tril(jnp.ones((length, length), BF16), -1)
        counts = dot(earlier, picks.astype(BF16)).astype(jnp.int32)
        rank = jnp.sum(jnp.where(picks, counts, 0), axis=-1)
        limit = jnp.sum(jnp.where(picks, limits[None, :], 0), axis=-1)
        slots = jnp.where(rank < limit, chosen * capacity + rank, slots_all)
        given.append((flags, gm, ge, along, chosen, slots))

    current = lax.dynamic_index_in_dim(stream, c, 0, keepdims=False).astype(F32)
    saved = []
    for layer in range(2):
        flags, gm, ge, along, chosen, slots = given[layer]
        scol, srow = slots.reshape(length, 1), slots.reshape(1, length)
        packed, mixed, middle, second, chances, sending = call_mixer(
            functools.partial(mixer_fwd, heads, experts),
            flags,
            (current, gm, ge, along, mcol, mrow, srow),
            weights[layer],
            [
                ((length, 3 * d), BF16),
                ((length, d), BF16),
                ((length, d), F32),
                ((length, d), BF16),
                ((length, 128), F32),
                ((slots_all, d), BF16),
            ],
            [],
        )
        rows = exchange(sending, n)
        output = call_ffn(ffn_fwd, flags, (rows,), (wi, wo), (wi_other, wo_other))
        back = exchange(output, n)
        hot = (jnp.arange(slots_all, dtype=jnp.int32)[None, :] == scol).astype(BF16)
        picked = dot(hot, back)
        lane = jnp.arange(128, dtype=jnp.int32)[None, :] == chosen[:, None]
        gate = jnp.sum(jnp.where(lane, chances, 0.0), axis=-1, keepdims=True)
        result = middle + gate * picked
        saved.append((current, packed, mixed, middle, second, chances, rows, picked, gate, lane))
        current = result.astype(BF16).astype(F32)
    final = result

    rows_mine = jnp.where(c == 0, saved[0][6], saved[1][6])
    rows_sent = swap(jnp.where(c == 0, saved[1][6], saved[0][6]), "section")
    rows_pair = jnp.concatenate([rows_mine, rows_sent], axis=0)
    rows_all = jnp.concatenate([rows_pair, swap(rows_pair, "shard")], axis=0)

    pull = lax.dynamic_index_in_dim(cotangent, c, 0, keepdims=False).astype(F32)
    pulls = [None, None]
    reduced = [None, None]
    rounds = n.bit_length()
    step, pair = 0, None
    for layer in (1, 0):
        flags, gm, ge, along, chosen, slots = given[layer]
        inputs, packed, mixed, middle, second, chances, rows, picked, gate, lane = saved[layer]
        scol, srow = slots.reshape(length, 1), slots.reshape(1, length)
        pull_gate = jnp.sum(pull * picked, axis=-1, keepdims=True)
        pull_logits = (chances * (jnp.where(lane, pull_gate, 0.0) - pull_gate * gate)).astype(BF16)
        pull_picked = (gate * pull).astype(BF16)
        hot = (jnp.arange(slots_all, dtype=jnp.int32)[:, None] == srow).astype(BF16)
        sending = dot(hot, pull_picked).astype(BF16)
        if layer == 0:
            part, sending = lax.optimization_barrier((added(pair), sending))
            pair = halve(part, 0)
        pulls[layer] = exchange(sending, n)
        back_rows = call_ffn(ffn_bwd, flags, (rows, pulls[layer]), (wi, wo), (wi_other, wo_other))
        if layer == 0:
            part, back_rows = lax.optimization_barrier((added(pair), back_rows))
            pair = halve(part, 1)
            pull_mine = jnp.where(c == 0, pulls[0], pulls[1])
            pull_sent = swap(jnp.where(c == 0, pulls[1], pulls[0]), "section")
        returned = exchange(back_rows, n)
        if layer == 1:
            rows_all, returned = lax.optimization_barrier((rows_all, returned))
        if layer == 0:
            part, pull_mine, pull_sent, returned = lax.optimization_barrier(
                (added(pair), pull_mine, pull_sent, returned)
            )
            pair = halve(part, 2)
            pull_pair = jnp.concatenate([pull_mine, pull_sent], axis=0)
            pull_all = jnp.concatenate([pull_pair, swap(pull_pair, "shard")], axis=0)
        d_inputs, keep, send, grid = call_mixer(
            functools.partial(mixer_bwd, heads, experts),
            flags,
            (pull, inputs, middle, second, packed, mixed, gm, ge, along, mcol, mrow, scol, pull_logits, returned),
            weights[layer],
            [
                ((length, d), F32),
                ((d, 2 * d + 128), BF16),
                ((d, 2 * d + 128), BF16),
                ((heads, length, length), BF16),
            ],
            [pltpu.VMEM((length, 3 * d), BF16)],
        )
        places = jnp.arange(length, dtype=jnp.int32)
        which = buckets(places[None, :] - places[:, None])
        each = (which[None] == jnp.arange(labels_n, dtype=jnp.int32)[:, None, None]).astype(BF16)
        grad_table = jnp.einsum("bij,hij->bh", each, grid, preferred_element_type=F32)
        devices = 2 * n
        padded = jnp.pad(
            grad_table.reshape(devices, -1), ((0, 0), (0, d // devices - table_size // devices))
        )
        spot = (0, 2 * d + experts + 2)
        column = padded.reshape(d, 1).astype(BF16)
        keep = lax.dynamic_update_slice(keep, column, spot)
        send = lax.dynamic_update_slice(send, column, spot)
        if layer == 1:
            pair = keep, swap(send, "section")
        else:
            for step in range(3, rounds):
                pair = halve(added(pair), step)
            reduced[1] = added(pair, F32)
            pair = keep, swap(send, "section")
            for step in range(rounds):
                pair = halve(added(pair), step)
                if step == 0:
                    grad_in, grad_out = call_grads(flags, rows_all, pull_all, wi, wo)
                    pair, grad_in = lax.optimization_barrier((pair, grad_in))
            reduced[0] = added(pair, F32)
        pull = d_inputs.astype(BF16).astype(F32)

    got = swap(jnp.where(c == 0, final, d_inputs), "section")
    ends = jnp.stack([jnp.where(c == 0, d_inputs, got), jnp.where(c == 0, got, final)])
    here = jnp.where(c == 0, reduced[0], reduced[1])
    there = swap(jnp.where(c == 0, reduced[1], reduced[0])[:, : 2 * d], "section")
    body = here[:, : 2 * d]
    total = jnp.concatenate(
        [jnp.where(c == 0, body, there), jnp.where(c == 0, there, body), here[:, 2 * d :]], axis=1
    )
    at = 4 * d + experts
    share = table_size // (2 * n)
    return (
        ends[None],
        total[None, :, : 3 * d],
        total[None, :, 3 * d : 4 * d],
        total[None, :share, at + 2],
        total[None, :, at],
        total[None, :, at + 1],
        total[None, :, 4 * d : at],
        grad_in[None, None],
        grad_out[None, None],
    )


def solution(mesh):
    placed = (
        P(None, ("expert", "shard"), None),
        P(None, ("expert", "shard"), None),
        P("section", None, ("expert", "shard"), None),
        P("section", None),
        P("section", "shard", None),
        P("section", "shard", None),
        P("section", None, None),
        P("section", None),
        P("section", None),
        P("section", "shard", None),
        P("section", "expert", None, None),
        P("section", "expert", None, None),
        P(None, ("expert", "shard"), None),
    )
    return jax.shard_map(
        shards,
        mesh=mesh,
        in_specs=placed,
        out_specs=(
            P("section", None, ("expert", "shard"), None),
            P("section", ("expert", "shard"), None),
            P("section", ("expert", "shard"), None),
            P("section", ("expert", "shard")),
            P("section", ("expert", "shard")),
            P("section", ("expert", "shard")),
            P("section", ("expert", "shard"), None),
            P("section", "expert", "shard", None),
            P("section", "expert", "shard", None),
        ),
        check_vma=False,
    )
```
